512 devices in a mesh: dp: 16 (over y, core), tensor: 32 (over z, x).
Axes of the slice: x: 4, y: 8, z: 8, core: 2. Of those that a mesh axis runs over, the one named last changes fastest.
Arguments:
- tokens: bfloat16 [2048, 4096], P('dp', 'tensor'), may hold values from -6 to 6
- gate_pre: bfloat16 [2048, 16384], P('dp', 'tensor'), may hold values from -6 to 6
- up_blocks: bfloat16 [32, 64, 128, 128], P('tensor'), may hold values from -0.125 to 0.125
- up_mask: int32 [32, 128], P(None, 'tensor'), may hold values from 0 to 1, as said below
- down_blocks: bfloat16 [32, 64, 128, 128], P('tensor'), may hold values from -0.0625 to 0.0625
- down_mask: int32 [128, 32], replicated, may hold values from 0 to 1, as said below
- down_owner: int32 [128], replicated, may hold values from 0 to 31, as said below
- cotangent: bfloat16 [2048, 4096], P('dp', 'tensor'), may hold values from -6 to 6
Outputs:
- mixed: bfloat16 [2048, 4096], P('dp', 'tensor')
- input_grad: bfloat16 [2048, 4096], P('dp', 'tensor')
- gate_grad: bfloat16 [2048, 16384], P('dp', 'tensor')
- up_grad: bfloat16 [32, 64, 128, 128], P('tensor', 'dp')
- down_grad: bfloat16 [32, 64, 128, 128], P('tensor', 'dp')
The draws below stay inside these ranges and needn't reach their ends.
Inputs may be any that keep to these rules, and one draw needn't show every extreme that they name: `up_mask`: each column strip of 4 block columns holds exactly 64 ones. `down_mask`: the rows owned by one device hold exactly 64 ones together. `down_owner`: every device owns exactly 4 block rows.
All inputs are finite; a program needn't handle non-finite values.
Results may differ from the reference program's by a relative error of at most 0.022.
Values may be sent and summed in bfloat16 or wider, within the bound.
No kernel may reach another device: no remote copies, remote signals or barrier semaphores. Data moves between devices by JAX's collectives and lax.ppermute only.
A program may use at most 128 MiB of HBM per device.

```python
import jax
import jax.numpy as jnp
from jax import lax

D = 4096
FF = 16384
BLK = 128
TOK = 128
TOKENS = 2048
DB = 32
FB = 128
STRIP = 4
KU = 64
KD = 64
N_DP = 16
N_TENSOR = 32


def down_layout_draw(key):
    key_perm, key_count, key_cols = jax.random.split(key, 3)
    ranking = jax.random.permutation(key_perm, FB)
    leading = jax.random.randint(key_count, (FB // 2,), 1, DB)
    slot_counts = jnp.stack([leading, DB - leading], axis=1).reshape(FB)
    counts = jnp.zeros((FB,), jnp.int32).at[ranking].set(slot_counts.astype(jnp.int32))
    owners = jnp.zeros((FB,), jnp.int32).at[ranking].set((jnp.arange(FB) // STRIP).astype(jnp.int32))
    subkeys = jax.random.split(key_cols, FB)
    col_ranks = jax.vmap(lambda sub_key: jax.random.permutation(sub_key, DB))(subkeys)
    kept = (col_ranks < counts[:, None]).astype(jnp.int32)
    return (kept, owners)


def draw_down_mask(key, part):
    return down_layout_draw(key)[0]


def draw_down_owner(key, part):
    return down_layout_draw(key)[1]


def draw_up_mask(key, part):
    key = jax.random.fold_in(key, 11)
    cells = DB * STRIP
    subkeys = jax.random.split(key, FB // STRIP)
    ranks = jax.vmap(lambda sub_key: jax.random.permutation(sub_key, cells))(subkeys)
    strips = (ranks < cells // 2).astype(jnp.int32).reshape(FB // STRIP, DB, STRIP)
    return jnp.transpose(strips, (1, 0, 2)).reshape(DB, FB)


def level_of(key, extent, shards, least, largest):
    def one(axis_at, shards_of):
        heights = jax.random.uniform(jax.random.fold_in(jax.random.fold_in(key, 6), axis_at), (shards_of,), jnp.float32, least / len(shards), largest / len(shards))
        return jnp.repeat(jnp.exp(heights), extent[axis_at] // shards_of).reshape((-1,) + (1,) * (len(extent) - axis_at - 1))

    level = one(*shards[0])
    for cut in shards[1:]:
        level = level * one(*cut)
    return level


def scatter_about(key, extent, scale, bound, pieces=(), held_as=jnp.bfloat16):
    array = scale * jax.random.normal(key, extent, jnp.float32)
    if pieces:
        array = array * level_of(key, extent, pieces, -0.22, 0.18)
    return jnp.clip(array, -bound, bound).astype(held_as)


def setup_inputs(seed: int = 0) -> dict:
    key_of = jax.random.split(jax.random.key(seed), 9)
    tokens = scatter_about(key_of[0], (TOKENS, D), 1.0, 6.0, ((0, 16), (1, 32)))
    gate_pre = scatter_about(key_of[1], (TOKENS, FF), 1.0, 6.0, ((0, 16), (1, 32)))
    up_blocks = scatter_about(key_of[2], (N_TENSOR, KU, BLK, BLK), (D // 2) ** -0.5, 0.125, ((0, 32),))
    up_mask = draw_up_mask(jax.random.fold_in(key_of[8], 71), 0)
    down_blocks = scatter_about(key_of[4], (N_TENSOR, KD, BLK, BLK), (FF // 2) ** -0.5, 0.0625, ((0, 32),))
    down_mask = draw_down_mask(jax.random.fold_in(key_of[8], 71), 0)
    down_owner = draw_down_owner(jax.random.fold_in(key_of[8], 71), 0)
    cotangent = scatter_about(key_of[7], (TOKENS, D), 1.0, 6.0, ((0, 16), (1, 32)))
    return dict(tokens=tokens, gate_pre=gate_pre, up_blocks=up_blocks, up_mask=up_mask, down_blocks=down_blocks, down_mask=down_mask, down_owner=down_owner, cotangent=cotangent)


def kept_positions(marked, total):
    marked = marked.reshape(-1).astype(jnp.int32)
    running = jnp.cumsum(marked) - 1
    target = jnp.where(marked > 0, running, total).astype(jnp.int32)
    indices = jnp.arange(marked.shape[0], dtype=jnp.int32)
    return jnp.zeros((total,), jnp.int32).at[target].set(indices, mode="drop")


def one_hot(indices, total):
    return (indices[:, None] == jnp.arange(total, dtype=jnp.int32)[None, :]).astype(jnp.float32)


def rounded(value):
    return lax.optimization_barrier(value.astype(jnp.bfloat16)).astype(jnp.float32)


def up_layout(up_mask, device):
    strip_mask = lax.dynamic_slice_in_dim(up_mask, device * STRIP, STRIP, 1)
    flat_pos = kept_positions(strip_mask, KU)
    return flat_pos // STRIP, flat_pos % STRIP


def down_layout(down_mask, down_owner, device):
    row_ids = kept_positions(down_owner == device, STRIP)
    owned_mask = jnp.take(down_mask, row_ids, axis=0)
    flat_pos = kept_positions(owned_mask, KD)
    return row_ids, flat_pos // DB, flat_pos % DB


def group_sum(left, right):
    left = left.reshape(N_DP, TOK, left.shape[1], left.shape[2])
    right = right.reshape(N_DP, TOK, right.shape[1], right.shape[2])
    terms = jnp.einsum('gnkb,gnkc->gkbc', left, right, precision=lax.Precision.HIGHEST)
    return jnp.sum(rounded(terms), axis=0)


def reference(tokens, gate_pre, up_blocks, up_mask, down_blocks, down_mask, down_owner, cotangent):
    total_tokens = tokens.shape[0]
    token_blocks = tokens.reshape(total_tokens, DB, BLK)
    cot_blocks = cotangent.reshape(total_tokens, DB, BLK)
    devices = jnp.arange(N_TENSOR, dtype=jnp.int32)

    def up_forward(device):
        row_ids, col_ids = up_layout(up_mask, device)
        weight = up_blocks[device].astype(jnp.float32)
        chosen = jnp.take(token_blocks, row_ids, axis=1).astype(jnp.float32)
        product = jnp.einsum('nkb,kbc->nkc', chosen, weight, precision=lax.Precision.HIGHEST)
        return jnp.einsum('nkc,ks->nsc', product, one_hot(col_ids, STRIP), precision=lax.Precision.HIGHEST)

    up_val = lax.map(up_forward, devices)
    up_val = jnp.transpose(up_val, (1, 0, 2, 3)).reshape(total_tokens, FB, BLK)
    gate_val = gate_pre.astype(jnp.float32).reshape(total_tokens, FB, BLK)
    sigmoid_gate = jax.nn.sigmoid(gate_val)
    activated = gate_val * sigmoid_gate
    hidden = (activated * up_val).astype(jnp.bfloat16)

    def down_step(output_sum, device):
        row_ids, slots, col_ids = down_layout(down_mask, down_owner, device)
        weight = down_blocks[device].astype(jnp.float32)
        h_owned = jnp.take(hidden, row_ids, axis=1)
        h_chosen = jnp.take(h_owned, slots, axis=1).astype(jnp.float32)
        product = jnp.einsum('nkb,kbc->nkc', h_chosen, weight, precision=lax.Precision.HIGHEST)
        partial_out = rounded(jnp.einsum('nkc,kj->njc', product, one_hot(col_ids, DB), precision=lax.Precision.HIGHEST))
        dy_chosen = jnp.take(cot_blocks, col_ids, axis=1).astype(jnp.float32)
        backward = jnp.einsum('nkc,kbc->nkb', dy_chosen, weight, precision=lax.Precision.HIGHEST)
        dh_owned = jnp.einsum('nkb,ka->nab', backward, one_hot(slots, STRIP), precision=lax.Precision.HIGHEST).astype(jnp.bfloat16)
        grad = group_sum(h_chosen, dy_chosen)
        return output_sum + partial_out, (row_ids, dh_owned, grad)

    start_out = jnp.zeros((total_tokens, DB, BLK), jnp.float32)
    output_sum, (all_rows, dh_stack, down_grad) = lax.scan(down_step, start_out, devices)
    mixed = output_sum.reshape(total_tokens, D).astype(jnp.bfloat16)
    dh_sorted = jnp.transpose(dh_stack, (1, 0, 2, 3)).reshape(total_tokens, FB, BLK)
    hidden_grad = jnp.zeros((total_tokens, FB, BLK), jnp.bfloat16).at[:, all_rows.reshape(-1)].set(dh_sorted)
    dh_float = hidden_grad.astype(jnp.float32)
    gate_grad = (dh_float * up_val * sigmoid_gate * (1.0 + gate_val * (1.0 - sigmoid_gate))).astype(jnp.bfloat16)
    gate_grad = gate_grad.reshape(total_tokens, FF)
    up_act_grad = (dh_float * activated).astype(jnp.bfloat16)

    def up_backward(input_sum, device):
        row_ids, col_ids = up_layout(up_mask, device)
        weight = up_blocks[device].astype(jnp.float32)
        du_strip = lax.dynamic_slice_in_dim(up_act_grad, device * STRIP, STRIP, 1)
        du_chosen = jnp.take(du_strip, col_ids, axis=1).astype(jnp.float32)
        product = jnp.einsum('nkc,kbc->nkb', du_chosen, weight, precision=lax.Precision.HIGHEST)
        partial_in = rounded(jnp.einsum('nkb,kr->nrb', product, one_hot(row_ids, DB), precision=lax.Precision.HIGHEST))
        chosen = jnp.take(token_blocks, row_ids, axis=1).astype(jnp.float32)
        return input_sum + partial_in, group_sum(chosen, du_chosen)

    start_in = jnp.zeros((total_tokens, DB, BLK), jnp.float32)
    input_sum, up_grad = lax.scan(up_backward, start_in, devices)
    input_grad = input_sum.reshape(total_tokens, D).astype(jnp.bfloat16)
    return mixed, input_grad, gate_grad, up_grad.astype(jnp.bfloat16), down_grad.astype(jnp.bfloat16)
```

```python
import jax
import jax.numpy as jnp
from jax import lax
from jax.experimental import pallas as pl
from jax.experimental.pallas import tpu as pltpu
from jax.sharding import PartitionSpec as P

BF = jnp.bfloat16
F32 = jnp.float32
VM = pl.BlockSpec(memory_space=pltpu.VMEM)
SM = pl.BlockSpec(memory_space=pltpu.SMEM)
ANY = pl.BlockSpec(memory_space=pl.ANY)
PARAMS = pltpu.CompilerParams(vmem_limit_bytes=56 * 1024 * 1024)
B = 128


def mm(a, b, dims=((1,), (0,))):
    return lax.dot_general(a, b, (dims, ((), ())), preferred_element_type=F32)


def dense_kernel(me, up_mask, down_mask, owner, w_up, w_down, wu, wd, up_pos, down_pos, sems):
    strip = up_mask.shape[1]
    wide = down_mask.shape[1]
    rows = down_mask.shape[0]
    kept = up_pos.shape[0]

    def clear(i, c):
        wu[pl.ds(pl.multiple_of(i * B, B), B), :] = jnp.zeros((B, wu.shape[1]), BF)
        return c

    lax.fori_loop(0, wu.shape[0] // B, clear, 0)
    for s in range(strip):
        for c in range(wd.shape[1] // 1024):
            wd[s * B : (s + 1) * B, c * 1024 : (c + 1) * 1024] = jnp.zeros((B, 1024), BF)

    def up_step(r, k):
        for c in range(strip):
            m = up_mask[r, c]

            @pl.when(m > 0)
            def _(k=k, c=c):
                kk = jnp.minimum(k, kept - 1)
                up_pos[kk] = r * strip + c
                pltpu.make_async_copy(
                    w_up.at[kk],
                    wu.at[pl.ds(pl.multiple_of(r * B, B), B), c * B : (c + 1) * B],
                    sems.at[0],
                ).start()

            k = k + jnp.where(m > 0, 1, 0)
        return k

    lax.fori_loop(0, up_mask.shape[0], up_step, 0)
    mine = me[0]

    def down_row(j, state):
        slot, k = state
        own = owner[j] == mine

        def walk(k):
            s = jnp.minimum(slot, strip - 1)

            def cell(c, k):
                m = down_mask[j, c]

                @pl.when(m > 0)
                def _():
                    kk = jnp.minimum(k, kept - 1)
                    down_pos[kk] = s * wide + c
                    pltpu.make_async_copy(
                        w_down.at[kk],
                        wd.at[pl.ds(pl.multiple_of(s * B, B), B), pl.ds(pl.multiple_of(c * B, B), B)],
                        sems.at[1],
                    ).start()

                return k + jnp.where(m > 0, 1, 0)

            return lax.fori_loop(0, wide, cell, k)

        k = lax.cond(own, walk, lambda k: k, k)
        return slot + jnp.where(own, 1, 0), k

    lax.fori_loop(0, rows, down_row, (0, 0))
    pltpu.make_async_copy(w_up, w_up, sems.at[0]).wait()
    pltpu.make_async_copy(w_down, w_down, sems.at[1]).wait()


def front_kernel(recv, wu, wd, gate, up_ref, send, acc, wide):
    n_src = recv.shape[0]
    tok = recv.shape[1] // 2
    hid = wu.shape[1]
    step = 4
    for i in range(0, n_src, step):
        x = jnp.concatenate([recv[i + j, :tok, :] for j in range(step)], axis=1)
        part = mm(x, wu[i * B : (i + step) * B, :])
        if i == 0:
            up_ref[...] = part
        else:
            up_ref[...] += part
    for i in range(0, n_src, step):
        y = jnp.concatenate([recv[i + j, tok:, :] for j in range(step)], axis=1)
        part = mm(y, wd[:, i * B : (i + step) * B], ((1,), (1,)))
        if i == 0:
            acc[...] = part
        else:
            acc[...] += part
    slices = send.shape[0]
    blocks = hid // B
    per = tok // slices
    for b in range(blocks):
        cols = slice(b * B, (b + 1) * B)
        g = gate[:, cols].astype(F32)
        h = (g * jax.nn.sigmoid(g) * up_ref[:, cols]).astype(BF).astype(F32)
        d = acc[:, cols].astype(BF).astype(F32)
        for q in range(per):
            rows = slice(q * slices, (q + 1) * slices)
            wide[:, b, q * B : (q + 1) * B] = h[rows, :]
            wide[:, blocks + b, q * B : (q + 1) * B] = d[rows, :]
    send[...] = wide[...].astype(BF)


def grads_kernel(up_pos, down_pos, got, up_ref, gate, recv, gate_grad, du, h_own, grads, wide, xt, ht, dub):
    n_src = recv.shape[0]
    tok = recv.shape[1] // 2
    slices = got.shape[0]
    blocks = gate.shape[1] // B
    per = tok // slices
    wide[...] = got[...].astype(F32)
    for b in range(blocks):
        cols = slice(b * B, (b + 1) * B)
        h = jnp.concatenate([wide[:, b, q * B : (q + 1) * B] for q in range(per)], axis=0)
        d = jnp.concatenate([wide[:, blocks + b, q * B : (q + 1) * B] for q in range(per)], axis=0)
        h_own[:, cols] = h.astype(BF)
        ht[b] = h.T.astype(BF)
        g = gate[:, cols].astype(F32)
        s = jax.nn.sigmoid(g)
        gate_grad[:, cols] = (d * up_ref[:, cols] * s * (1.0 + g * (1.0 - s))).astype(BF)
        u = (d * (g * s)).astype(BF)
        du[:, cols] = u
        dub[b] = u

    def turn(i, c):
        xt[i] = recv[i, :tok, :].T
        return c

    lax.fori_loop(0, n_src, turn, 0)
    groups = grads.shape[0]
    each = grads.shape[2]
    wide_blocks = n_src

    def block(i, c):
        for j in range(each):
            k = i * each + j
            p = up_pos[k]
            grads[i, 0, j] = mm(xt[p // blocks], dub[lax.rem(p, blocks)]).astype(BF)
            p = down_pos[k]
            grads[i, 1, j] = mm(ht[p // wide_blocks], recv[lax.rem(p, wide_blocks), tok:, :]).astype(BF)
        return c

    lax.fori_loop(0, groups, block, 0)


def parts_kernel(h_own, du, wu, wd, parts):
    n_dst = parts.shape[0]
    tok = parts.shape[1] // 2
    step = 4
    h = h_own[...]
    u = du[...]
    for i in range(0, n_dst, step):
        o = mm(h, wd[:, i * B : (i + step) * B]).astype(BF)
        g = mm(u, wu[i * B : (i + step) * B, :], ((1,), (1,))).astype(BF)
        for j in range(step):
            parts[i + j, :tok, :] = o[:, j * B : (j + 1) * B]
            parts[i + j, tok:, :] = g[:, j * B : (j + 1) * B]


def sum_kernel(pieces, mixed, input_grad):
    tok = mixed.shape[0]
    for out, base in ((mixed, 0), (input_grad, tok)):
        for r in range(0, tok, 32):
            total = pieces[0, base + r : base + r + 32, :].astype(F32)
            for i in range(1, pieces.shape[0]):
                total += pieces[i, base + r : base + r + 32, :].astype(F32)
            out[r : r + 32, :] = total.astype(BF)


def exchange(x):
    return lax.all_to_all(x, "tensor", split_axis=0, concat_axis=0, tiled=True)


def route_matrix(owner, devices):
    count = owner.shape[0]
    per = count // devices
    ids = jnp.arange(count, dtype=jnp.int32)
    same = (owner[:, None] == owner[None, :]) & (ids[None, :] < ids[:, None])
    home = owner * per + jnp.sum(same.astype(jnp.int32), axis=1)
    both = jnp.broadcast_to(home.reshape(devices, 1, per), (devices, 2, per)).reshape(-1)
    at = jnp.arange(2 * count, dtype=jnp.int32)
    ident = (at // (2 * per)) * per + at % per
    kind = (at // per) % 2
    forth = both[None, :] == ident[:, None]
    back = both[:, None] == ident[None, :]
    keep = kind[:, None] == kind[None, :]
    return (keep & jnp.where(kind[:, None] == 0, forth, back)).astype(BF)


def shards(tokens, gate_pre, up_blocks, up_mask, down_blocks, down_mask, down_owner, cotangent):
    devices = lax.axis_size("tensor")
    groups = lax.axis_size("dp")
    tok, width = tokens.shape
    hid = gate_pre.shape[1]
    model = devices * width
    kept = up_blocks.shape[1]
    sds = jax.ShapeDtypeStruct

    both = jnp.concatenate([tokens, cotangent], axis=0)
    recv = exchange(jnp.broadcast_to(both[None], (devices, 2 * tok, width)))

    me = lax.axis_index("tensor").astype(jnp.int32).reshape(1)
    wu, wd, up_pos, down_pos = pl.pallas_call(
        dense_kernel,
        out_shape=(
            sds((model, hid), BF),
            sds((hid, model), BF),
            sds((kept,), jnp.int32),
            sds((kept,), jnp.int32),
        ),
        in_specs=[SM, SM, SM, SM, ANY, ANY],
        out_specs=(VM, VM, SM, SM),
        scratch_shapes=[pltpu.SemaphoreType.DMA((2,))],
        compiler_params=PARAMS,
        name="dense",
    )(me, up_mask, down_mask, down_owner, up_blocks[0], down_blocks[0])

    rows = 2 * hid // B
    lanes = tok // devices * B
    up, send = pl.pallas_call(
        front_kernel,
        out_shape=(sds((tok, hid), F32), sds((devices, rows, lanes), BF)),
        in_specs=[VM] * 4,
        out_specs=(VM, VM),
        scratch_shapes=[pltpu.VMEM((tok, hid), F32), pltpu.VMEM((devices, rows, lanes), F32)],
        compiler_params=PARAMS,
        name="front",
    )(recv, wu, wd, gate_pre)

    route = route_matrix(down_owner, devices)
    turned = exchange(send).reshape(devices * rows, lanes)
    turned = jnp.dot(route, turned, preferred_element_type=F32).astype(BF)
    got = exchange(turned.reshape(devices, rows, lanes))

    each = kept // groups
    gate_grad, du, h_own, grads = pl.pallas_call(
        grads_kernel,
        out_shape=(
            sds((tok, hid), BF),
            sds((tok, hid), BF),
            sds((tok, hid), BF),
            sds((groups, 2, each, B, B), BF),
        ),
        in_specs=[SM, SM] + [VM] * 4,
        out_specs=(VM,) * 4,
        scratch_shapes=[
            pltpu.VMEM((devices, rows, lanes), F32),
            pltpu.VMEM((devices, B, tok), BF),
            pltpu.VMEM((hid // B, B, tok), BF),
            pltpu.VMEM((hid // B, tok, B), BF),
        ],
        compiler_params=PARAMS,
        name="grads",
    )(up_pos, down_pos, got, up, gate_pre, recv)

    summed = lax.psum_scatter(grads, "dp", scatter_dimension=0, tiled=True)

    parts = pl.pallas_call(
        parts_kernel,
        out_shape=sds((devices, 2 * tok, width), BF),
        in_specs=[VM] * 4,
        out_specs=VM,
        compiler_params=PARAMS,
        name="parts",
    )(h_own, du, wu, wd)
    pieces = exchange(parts)
    mixed, input_grad = pl.pallas_call(
        sum_kernel,
        out_shape=(sds((tok, width), BF), sds((tok, width), BF)),
        in_specs=[VM],
        out_specs=(VM, VM),
        compiler_params=PARAMS,
        name="sums",
    )(pieces)
    return mixed, input_grad, gate_grad, summed[:, 0], summed[:, 1]


def solution(mesh):
    placed = (
        P("dp", "tensor"),
        P("dp", "tensor"),
        P("tensor", None, None, None),
        P(None, "tensor"),
        P("tensor", None, None, None),
        P(),
        P(),
        P("dp", "tensor"),
    )
    return jax.shard_map(
        shards,
        mesh=mesh,
        in_specs=placed,
        out_specs=(
            P("dp", "tensor"),
            P("dp", "tensor"),
            P("dp", "tensor"),
            P("tensor", "dp", None, None),
            P("tensor", "dp", None, None),
        ),
        check_vma=False,
    )
```

```python
import functools

import jax
import jax.numpy as jnp
from jax import lax
from jax.experimental import pallas as pl
from jax.experimental.pallas import tpu as pltpu
from jax.sharding import PartitionSpec as P


BF = jnp.bfloat16
F32 = jnp.float32
VM = pl.BlockSpec(memory_space=pltpu.VMEM)
SM = pl.BlockSpec(memory_space=pltpu.SMEM)
ANY = pl.BlockSpec(memory_space=pl.ANY)


def params(mib):
    return pltpu.CompilerParams(vmem_limit_bytes=mib * 1024 * 1024)


B = 128
INNER = 4


def mm(a, b, dims=((1,), (0,))):
    return lax.dot_general(a, b, (dims, ((), ())), preferred_element_type=F32)


def dense_kernel(me, up_mask, down_mask, owner, w_up, w_down, wu, wd, route, up_pos, down_pos, ones, filled, sems, inner):
    wide, strip = up_mask.shape
    rows = down_mask.shape[0]
    kept = up_pos.shape[0]
    outer = wide // inner

    mine = me[0]

    def place(r):
        return lax.rem(lax.rem(r, inner) + inner - lax.rem(mine, inner), inner) * outer + r // inner

    for ref in (wu, wd):
        for s in range(strip):
            for c in range(ref.shape[1] // 1024):
                ref[s * B : (s + 1) * B, c * 1024 : (c + 1) * 1024] = jnp.zeros((B, 1024), BF)

    def down_row(j, state):
        slot, k = state
        own = owner[j] == mine

        def walk(k):
            s = jnp.minimum(slot, strip - 1)

            def cell(c, k):
                m = down_mask[j, c]

                @pl.when(m > 0)
                def _():
                    kk = jnp.minimum(k, kept - 1)
                    at = place(c)
                    down_pos[kk] = s * wide + at
                    pltpu.make_async_copy(
                        w_down.at[kk],
                        wd.at[pl.ds(pl.multiple_of(s * B, B), B), pl.ds(pl.multiple_of(at * B, B), B)],
                        sems.at[0],
                    ).start()

                return k + jnp.where(m > 0, 1, 0)

            return lax.fori_loop(0, wide, cell, k)

        k = lax.cond(own, walk, lambda k: k, k)
        return slot + jnp.where(own, 1, 0), k

    lax.fori_loop(0, rows, down_row, (0, 0))

    def up_step(r, k):
        at = place(r) * strip
        for c in range(strip):
            m = up_mask[r, c]

            @pl.when(m > 0)
            def _(k=k, c=c):
                up_pos[jnp.minimum(k, kept - 1)] = at + c

            k = k + jnp.where(m > 0, 1, 0)
        return k

    lax.fori_loop(0, wide, up_step, 0)

    def turn(i, carry):
        for j in range(8):
            k = i * 8 + j
            p = up_pos[k]
            r = pl.multiple_of(p // strip * B, B)
            c = pl.multiple_of(lax.rem(p, strip) * B, B)
            wu[pl.ds(c, B), pl.ds(r, B)] = w_up[k].T
        return carry

    lax.fori_loop(0, kept // 8, turn, 0)

    for t in range(wide):
        filled[t] = 0
    lane = lax.broadcasted_iota(jnp.int32, (1, ones.shape[1]), 1)

    def line(i, carry):
        to = jnp.clip(owner[i], 0, wide - 1)
        n = jnp.minimum(filled[to], strip - 1)
        filled[to] = n + 1
        there = to * 2 * strip + n
        here = i // strip * 2 * strip + lax.rem(i, strip)
        ones[pl.ds(there, 1), :] = jnp.where(lane == here, 1.0, 0.0)
        ones[pl.ds(here + strip, 1), :] = jnp.where(lane == there + strip, 1.0, 0.0)
        return carry

    lax.fori_loop(0, rows, line, 0)
    route[...] = ones[...].astype(BF)
    pltpu.make_async_copy(w_down, w_down, sems.at[0]).wait()


def front_kernel(r0, r1, r2, r3, wu, wd, gate, up_ref, send, far, acc_u, acc, wide):
    outer, tok = r0.shape[0], r0.shape[1] // 2
    hid = wu.shape[0]
    for n, recv in enumerate((r0, r1, r2, r3)):
        if n > 0:
            far[(n - 1) * outer : n * outer] = recv[...]
        cols = slice(n * outer * B, (n + 1) * outer * B)
        x = jnp.concatenate([recv[i, :tok, :] for i in range(outer)], axis=0)
        y = jnp.concatenate([recv[i, tok:, :] for i in range(outer)], axis=1)
        u = mm(wu[:, cols], x)
        d = mm(y, wd[:, cols], ((1,), (1,)))
        if n == 0:
            acc_u[...] = u
            acc[...] = d
        else:
            acc_u[...] += u
            acc[...] += d
    for b in range(hid // B):
        up_ref[:, b * B : (b + 1) * B] = acc_u[b * B : (b + 1) * B, :].T
    slices = send.shape[0]
    blocks = hid // B
    per = tok // slices
    for b in range(blocks):
        cols = slice(b * B, (b + 1) * B)
        g = gate[:, cols].astype(F32)
        h = (g * jax.nn.sigmoid(g) * up_ref[:, cols]).astype(BF).astype(F32)
        d = acc[:, cols].astype(BF).astype(F32)
        for q in range(per):
            rows = slice(q * slices, (q + 1) * slices)
            wide[:, b, q * B : (q + 1) * B] = h[rows, :]
            wide[:, blocks + b, q * B : (q + 1) * B] = d[rows, :]
    send[...] = wide[...].astype(BF)


def spread_kernel(tokens_in, cotangent_in, out, tokens, cotangent, sems):
    width = tokens.shape[1]
    first = pltpu.make_async_copy(tokens_in, tokens, sems.at[0])
    second = pltpu.make_async_copy(cotangent_in, cotangent, sems.at[1])
    first.start()
    second.start()
    first.wait()
    second.wait()
    x = tokens[...].astype(F32).T.astype(BF)
    y = cotangent[...]
    for i in range(out.shape[0]):
        out[i, :width, :] = x
        out[i, width:, :] = y


def back_kernel(got, up_ref, gate, gate_grad, du, h_own, swap, wide):
    slices = got.shape[0]
    blocks = gate.shape[1] // B
    per = gate.shape[0] // slices
    wide[...] = got[...].astype(F32)
    for b in range(blocks):
        cols = slice(b * B, (b + 1) * B)
        h = jnp.concatenate([wide[:, b, q * B : (q + 1) * B] for q in range(per)], axis=0)
        d = jnp.concatenate([wide[:, blocks + b, q * B : (q + 1) * B] for q in range(per)], axis=0)
        h_own[:, cols] = h.astype(BF)
        swap[blocks + b] = h.T.astype(BF)
        g = gate[:, cols].astype(F32)
        s = jax.nn.sigmoid(g)
        gate_grad[:, cols] = (d * up_ref[:, cols] * s * (1.0 + g * (1.0 - s))).astype(BF)
        u = (d * (g * s)).astype(BF)
        du[:, cols] = u
        swap[b] = u


def grads_kernel(core, up_pos, down_pos, near, far, near2, far2, swap, swap2, grads, full, full2, du, ht, sems):
    outer = near.shape[0]
    n_src = full.shape[0]
    tok = full.shape[1] // 2
    blocks = du.shape[0]
    moves = []
    for t, (src, dst) in enumerate(
        ((near, full.at[:outer]), (far, full.at[outer:]), (near2, full2.at[:outer]), (far2, full2.at[outer:]))
    ):
        move = pltpu.make_async_copy(src, dst, sems.at[t])
        move.start()
        moves.append(move)
    for b in range(blocks):
        du[b, :tok, :] = swap[b]
        du[b, tok:, :] = swap2[b]
        ht[b, :, :tok] = swap[blocks + b]
        ht[b, :, tok:] = swap2[blocks + b]
    for move in moves:
        move.wait()
    each = grads.shape[2]

    def block(i, c):
        for j in range(each):
            k = (2 * i + core[0]) * each + j
            p = up_pos[k]
            r = p // blocks
            xt = jnp.concatenate([full[r, :tok, :], full2[r, :tok, :]], axis=1)
            grads[i, 0, j] = mm(xt, du[lax.rem(p, blocks)]).astype(BF)
            p = down_pos[k]
            r = lax.rem(p, n_src)
            y = jnp.concatenate([full[r, tok:, :], full2[r, tok:, :]], axis=0)
            grads[i, 1, j] = mm(ht[p // n_src], y).astype(BF)
        return c

    lax.fori_loop(0, grads.shape[0], block, 0)


def parts_kernel(me, h_own, du, wu_in, wd_in, parts, done, wu, wd, sems):
    inner, outer = parts.shape[:2]
    tok = parts.shape[2] // 2
    copies = []
    for n in range(inner):
        cols = slice(n * outer * B, (n + 1) * outer * B)
        pair = []
        for t, (src, dst) in enumerate(((wu_in, wu), (wd_in, wd))):
            copy = pltpu.make_async_copy(src.at[:, cols], dst.at[:, cols], sems.at[t, n])
            copy.start()
            pair.append(copy)
        copies.append(pair)
    h = h_own[...]
    u = du[...]
    for n, (cu, cd) in enumerate(copies):
        cols = slice(n * outer * B, (n + 1) * outer * B)
        to = lax.rem(me[0] + n, inner)
        cu.wait()
        g = mm(u, wu[:, cols]).astype(BF)
        cd.wait()
        o = mm(h, wd[:, cols]).astype(BF)
        for j in range(outer):
            parts[to, j, :tok, :] = o[:, j * B : (j + 1) * B]
            parts[to, j, tok:, :] = g[:, j * B : (j + 1) * B]
    done[...] = jnp.zeros_like(done)


def add_up(pieces, at):
    total = pieces[(0,) + at].astype(F32)
    for i in range(1, pieces.shape[0]):
        total += pieces[(i,) + at].astype(F32)
    return total.astype(BF)


def first_sum_kernel(pieces, out):
    for j in range(out.shape[0]):
        out[j] = add_up(pieces, (j,))


def sum_kernel(pieces, mixed, input_grad):
    tok = mixed.shape[0]
    for out, base in ((mixed, 0), (input_grad, tok)):
        for r in range(0, tok, 32):
            out[r : r + 32, :] = add_up(pieces, (slice(base + r, base + r + 32),))


def exchange(x, teams=None):
    return lax.all_to_all(x, "tensor", split_axis=0, concat_axis=0, tiled=True, axis_index_groups=teams)


def turn_kernel(route, came, goes):
    n, rows, lanes = came.shape
    flat = came[...].astype(F32).reshape(n * rows, lanes).astype(BF)
    goes[...] = mm(route[...], flat).reshape(n, rows, lanes).astype(BF)


def shards(
    inner, tokens, gate_pre, up_blocks, up_mask, down_blocks, down_mask, down_owner, cotangent
):
    devices = lax.axis_size("tensor")
    groups = lax.axis_size("dp")
    tok, width = tokens.shape
    hid = gate_pre.shape[1]
    model = devices * width
    kept = up_blocks.shape[1]
    sds = jax.ShapeDtypeStruct

    outer = devices // inner
    along_x = [[z * inner + x for x in range(inner)] for z in range(outer)]
    along_z = [[z * inner + x for z in range(outer)] for x in range(inner)]
    spread = pl.pallas_call(
        spread_kernel,
        out_shape=sds((outer, 2 * tok, width), BF),
        in_specs=[ANY, ANY],
        out_specs=VM,
        scratch_shapes=[
            pltpu.VMEM((tok, width), BF),
            pltpu.VMEM((tok, width), BF),
            pltpu.SemaphoreType.DMA((2,)),
        ],
        compiler_params=params(60),
        name="spread",
    )(tokens, cotangent)
    def shift(x, by):
        pairs = [(z * inner + i, z * inner + (i + by) % inner) for z in range(outer) for i in range(inner)]
        return lax.ppermute(x, "tensor", pairs)

    me = lax.axis_index("tensor").astype(jnp.int32).reshape(1)
    wu, wd, route, up_pos, down_pos = pl.pallas_call(
        functools.partial(dense_kernel, inner=inner),
        out_shape=(
            sds((hid, model), BF),
            sds((hid, model), BF),
            sds((2 * hid // B * devices, 2 * hid // B * devices), BF),
            sds((kept,), jnp.int32),
            sds((kept,), jnp.int32),
        ),
        in_specs=[SM, SM, SM, SM, VM, ANY],
        out_specs=(VM, VM, VM, SM, SM),
        scratch_shapes=[
            pltpu.VMEM((2 * hid // B * devices, 2 * hid // B * devices), F32),
            pltpu.SMEM((devices,), jnp.int32),
            pltpu.SemaphoreType.DMA((1,)),
        ],
        cost_estimate=pl.CostEstimate(flops=0, bytes_accessed=24 << 20, transcendentals=0),
        compiler_params=params(16),
        name="dense",
    )(me, up_mask, down_mask, down_owner, up_blocks[0], down_blocks[0])

    near = exchange(spread, along_z)
    pieces = [near] + [shift(near, -j) for j in range(1, inner)]
    pairs = [(i, i ^ 1) for i in range(groups)]
    late, up_pos = lax.optimization_barrier((near, up_pos))
    near2 = lax.ppermute(late, "dp", pairs)

    rows = 2 * hid // B
    lanes = tok // devices * B
    up, send, far = pl.pallas_call(
        front_kernel,
        out_shape=(
            sds((tok, hid), F32),
            sds((devices, rows, lanes), BF),
            sds((devices - outer, 2 * tok, width), BF),
        ),
        in_specs=[VM] * 7,
        out_specs=(VM,) * 3,
        scratch_shapes=[
            pltpu.VMEM((hid, tok), F32),
            pltpu.VMEM((tok, hid), F32),
            pltpu.VMEM((devices, rows, lanes), F32),
        ],
        compiler_params=params(16),
        name="front",
    )(*pieces, wu, wd, gate_pre)

    send, near2 = lax.optimization_barrier((send, near2))
    turned = pl.pallas_call(
        turn_kernel,
        out_shape=sds((devices, rows, lanes), BF),
        in_specs=[VM, VM],
        out_specs=VM,
        compiler_params=params(4),
        name="turn",
    )(route, exchange(send))
    got = exchange(turned)
    far2 = lax.ppermute(far, "dp", pairs)

    each = kept // groups
    blocks = hid // B
    gate_grad, du, h_own, swap = pl.pallas_call(
        back_kernel,
        out_shape=(
            sds((tok, hid), BF),
            sds((tok, hid), BF),
            sds((tok, hid), BF),
            sds((2 * blocks, B, B), BF),
        ),
        in_specs=[VM] * 3,
        out_specs=(VM,) * 4,
        scratch_shapes=[pltpu.VMEM((devices, rows, lanes), F32)],
        compiler_params=params(6),
        name="back",
    )(got, up, gate_pre)
    swap2 = lax.ppermute(swap, "dp", pairs)

    parts, done = pl.pallas_call(
        parts_kernel,
        out_shape=(sds((inner, outer, 2 * tok, width), BF), sds((8, B), F32)),
        in_specs=[SM, VM, VM, ANY, ANY],
        out_specs=(VM, VM),
        scratch_shapes=[
            pltpu.VMEM((hid, model), BF),
            pltpu.VMEM((hid, model), BF),
            pltpu.SemaphoreType.DMA((2, inner)),
        ],
        compiler_params=params(60),
        cost_estimate=pl.CostEstimate(flops=4 * tok * hid * model, bytes_accessed=10 << 20, transcendentals=0),
        name="parts",
    )(me, h_own, du, wu, wd)
    done, swap2 = lax.optimization_barrier((done, swap2))

    core = lax.rem(lax.axis_index("dp"), 2).astype(jnp.int32).reshape(1)
    grads = pl.pallas_call(
        grads_kernel,
        out_shape=sds((groups // 2, 2, each, B, B), BF),
        in_specs=[SM] * 3 + [ANY] * 4 + [VM] * 2,
        out_specs=VM,
        scratch_shapes=[
            pltpu.VMEM((devices, 2 * tok, width), BF),
            pltpu.VMEM((devices, 2 * tok, width), BF),
            pltpu.VMEM((blocks, 2 * tok, B), BF),
            pltpu.VMEM((blocks, B, 2 * tok), BF),
            pltpu.SemaphoreType.DMA((4,)),
        ],
        compiler_params=params(12),
        cost_estimate=pl.CostEstimate(flops=2 * kept * 2 * tok * B * B, bytes_accessed=8 << 20, transcendentals=0),
        name="grads",
    )(core, up_pos, down_pos, near, far, near2, far2, swap, swap2)
    parts, grads = lax.optimization_barrier((parts, grads))
    columns = [[y * 2 + c for y in range(groups // 2)] for c in range(2)]
    summed = lax.psum_scatter(grads, "dp", scatter_dimension=0, tiled=True, axis_index_groups=columns)

    first = pl.pallas_call(
        first_sum_kernel,
        out_shape=sds((outer, 2 * tok, width), BF),
        in_specs=[VM],
        out_specs=VM,
        compiler_params=params(8),
        name="first_sums",
    )(exchange(parts, along_x))
    pieces = exchange(first, along_z)
    mixed, input_grad = pl.pallas_call(
        sum_kernel,
        out_shape=(sds((tok, width), BF), sds((tok, width), BF)),
        in_specs=[VM],
        out_specs=(VM, VM),
        compiler_params=params(6),
        name="sums",
    )(pieces)
    return mixed, input_grad, gate_grad, summed[:, 0], summed[:, 1]


def solution(mesh):
    placed = (
        P("dp", "tensor"),
        P("dp", "tensor"),
        P("tensor", None, None, None),
        P(None, "tensor"),
        P("tensor", None, None, None),
        P(),
        P(),
        P("dp", "tensor"),
    )
    return jax.shard_map(
        functools.partial(shards, INNER),
        mesh=mesh,
        in_specs=placed,
        out_specs=(
            P("dp", "tensor"),
            P("dp", "tensor"),
            P("dp", "tensor"),
            P("tensor", "dp", None, None),
            P("tensor", "dp", None, None),
        ),
        check_vma=False,
    )
```

```python
import functools

import jax
import jax.numpy as jnp
from jax import lax
from jax.experimental import pallas as pl
from jax.experimental.pallas import tpu as pltpu
from jax.sharding import PartitionSpec as P


BF = jnp.bfloat16
F32 = jnp.float32
VM = pl.BlockSpec(memory_space=pltpu.VMEM)
SM = pl.BlockSpec(memory_space=pltpu.SMEM)
ANY = pl.BlockSpec(memory_space=pl.ANY)


def params(mib):
    return pltpu.CompilerParams(vmem_limit_bytes=mib * 1024 * 1024)


B = 128
INNER = 4


def mm(a, b, dims=((1,), (0,))):
    return lax.dot_general(a, b, (dims, ((), ())), preferred_element_type=F32)


def dense_kernel(me, up_mask, down_mask, owner, w_up, w_down, wu, wd, route, up_pos, down_pos, ones, filled, sems, inner):
    wide, strip = up_mask.shape
    rows = down_mask.shape[0]
    kept = up_pos.shape[0]
    outer = wide // inner

    mine = me[0]

    def place(r):
        return lax.rem(lax.rem(r, inner) + inner - lax.rem(mine, inner), inner) * outer + r // inner

    for ref in (wu, wd):
        for s in range(strip):
            for c in range(ref.shape[1] // 1024):
                ref[s * B : (s + 1) * B, c * 1024 : (c + 1) * 1024] = jnp.zeros((B, 1024), BF)

    def down_row(j, state):
        slot, k = state
        own = owner[j] == mine

        def walk(k):
            s = jnp.minimum(slot, strip - 1)

            def cell(c, k):
                m = down_mask[j, c]

                @pl.when(m > 0)
                def _():
                    kk = jnp.minimum(k, kept - 1)
                    at = place(c)
                    down_pos[kk] = s * wide + at
                    pltpu.make_async_copy(
                        w_down.at[kk],
                        wd.at[pl.ds(pl.multiple_of(s * B, B), B), pl.ds(pl.multiple_of(at * B, B), B)],
                        sems.at[0],
                    ).start()

                return k + jnp.where(m > 0, 1, 0)

            return lax.fori_loop(0, wide, cell, k)

        k = lax.cond(own, walk, lambda k: k, k)
        return slot + jnp.where(own, 1, 0), k

    lax.fori_loop(0, rows, down_row, (0, 0))

    def up_step(r, k):
        at = place(r) * strip
        for c in range(strip):
            m = up_mask[r, c]

            @pl.when(m > 0)
            def _(k=k, c=c):
                up_pos[jnp.minimum(k, kept - 1)] = at + c

            k = k + jnp.where(m > 0, 1, 0)
        return k

    lax.fori_loop(0, wide, up_step, 0)

    def turn(i, carry):
        for j in range(8):
            k = i * 8 + j
            p = up_pos[k]
            r = pl.multiple_of(p // strip * B, B)
            c = pl.multiple_of(lax.rem(p, strip) * B, B)
            wu[pl.ds(c, B), pl.ds(r, B)] = w_up[k].T
        return carry

    lax.fori_loop(0, kept // 8, turn, 0)

    for t in range(wide):
        filled[t] = 0
    lane = lax.broadcasted_iota(jnp.int32, (1, ones.shape[1]), 1)

    def line(i, carry):
        to = jnp.clip(owner[i], 0, wide - 1)
        n = jnp.minimum(filled[to], strip - 1)
        filled[to] = n + 1
        there = to * 2 * strip + n
        here = i // strip * 2 * strip + lax.rem(i, strip)
        ones[pl.ds(there, 1), :] = jnp.where(lane == here, 1.0, 0.0)
        ones[pl.ds(here + strip, 1), :] = jnp.where(lane == there + strip, 1.0, 0.0)
        return carry

    lax.fori_loop(0, rows, line, 0)
    route[...] = ones[...].astype(BF)
    pltpu.make_async_copy(w_down, w_down, sems.at[0]).wait()


def front_kernel(r0, r1, r2, r3, wu, wd, gate, up_ref, send, far, acc_u, acc, wide):
    outer, tok = r0.shape[0], r0.shape[1] // 2
    hid = wu.shape[0]
    for n, recv in enumerate((r0, r1, r2, r3)):
        if n > 0:
            far[(n - 1) * outer : n * outer] = recv[...]
        cols = slice(n * outer * B, (n + 1) * outer * B)
        x = jnp.concatenate([recv[i, :tok, :] for i in range(outer)], axis=0)
        y = jnp.concatenate([recv[i, tok:, :] for i in range(outer)], axis=1)
        u = mm(wu[:, cols], x)
        d = mm(y, wd[:, cols], ((1,), (1,)))
        if n == 0:
            acc_u[...] = u
            acc[...] = d
        else:
            acc_u[...] += u
            acc[...] += d
    for b in range(hid // B):
        up_ref[:, b * B : (b + 1) * B] = acc_u[b * B : (b + 1) * B, :].T
    slices = send.shape[0]
    blocks = hid // B
    per = tok // slices
    for b in range(blocks):
        cols = slice(b * B, (b + 1) * B)
        g = gate[:, cols].astype(F32)
        h = (g * jax.nn.sigmoid(g) * up_ref[:, cols]).astype(BF).astype(F32)
        d = acc[:, cols].astype(BF).astype(F32)
        for q in range(per):
            rows = slice(q * slices, (q + 1) * slices)
            wide[:, b, q * B : (q + 1) * B] = h[rows, :]
            wide[:, blocks + b, q * B : (q + 1) * B] = d[rows, :]
    send[...] = wide[...].astype(BF)


def spread_kernel(tokens_in, cotangent_in, out, tokens, cotangent, sems):
    width = tokens.shape[1]
    first = pltpu.make_async_copy(tokens_in, tokens, sems.at[0])
    second = pltpu.make_async_copy(cotangent_in, cotangent, sems.at[1])
    first.start()
    second.start()
    first.wait()
    second.wait()
    x = tokens[...].astype(F32).T.astype(BF)
    y = cotangent[...]
    for i in range(out.shape[0]):
        out[i, :width, :] = x
        out[i, width:, :] = y


def back_kernel(got, up_ref, gate, gate_grad, du, h_own, swap, wide):
    slices = got.shape[0]
    blocks = gate.shape[1] // B
    per = gate.shape[0] // slices
    wide[...] = got[...].astype(F32)
    for b in range(blocks):
        cols = slice(b * B, (b + 1) * B)
        h = jnp.concatenate([wide[:, b, q * B : (q + 1) * B] for q in range(per)], axis=0)
        d = jnp.concatenate([wide[:, blocks + b, q * B : (q + 1) * B] for q in range(per)], axis=0)
        h_own[:, cols] = h.astype(BF)
        swap[blocks + b] = h.T.astype(BF)
        g = gate[:, cols].astype(F32)
        s = jax.nn.sigmoid(g)
        gate_grad[:, cols] = (d * up_ref[:, cols] * s * (1.0 + g * (1.0 - s))).astype(BF)
        u = (d * (g * s)).astype(BF)
        du[:, cols] = u
        swap[b] = u


def grads_kernel(core, up_pos, down_pos, near, far, near2, far2, swap, swap2, grads, full, full2, du, ht, sems):
    outer = near.shape[0]
    n_src = full.shape[0]
    tok = full.shape[1] // 2
    blocks = du.shape[0]
    moves = []
    for t, (src, dst) in enumerate(
        ((near, full.at[:outer]), (far, full.at[outer:]), (near2, full2.at[:outer]), (far2, full2.at[outer:]))
    ):
        move = pltpu.make_async_copy(src, dst, sems.at[t])
        move.start()
        moves.append(move)
    for b in range(blocks):
        du[b, :tok, :] = swap[b]
        du[b, tok:, :] = swap2[b]
        ht[b, :, :tok] = swap[blocks + b]
        ht[b, :, tok:] = swap2[blocks + b]
    for move in moves:
        move.wait()
    each = grads.shape[2]

    def block(i, c):
        for j in range(each):
            k = (2 * i + core[0]) * each + j
            p = up_pos[k]
            r = p // blocks
            xt = jnp.concatenate([full[r, :tok, :], full2[r, :tok, :]], axis=1)
            grads[i, 0, j] = mm(xt, du[lax.rem(p, blocks)]).astype(BF)
            p = down_pos[k]
            r = lax.rem(p, n_src)
            y = jnp.concatenate([full[r, tok:, :], full2[r, tok:, :]], axis=0)
            grads[i, 1, j] = mm(ht[p // n_src], y).astype(BF)
        return c

    lax.fori_loop(0, grads.shape[0], block, 0)


def parts_kernel(me, h_own, du, wu, wd, parts, done):
    inner, outer = parts.shape[:2]
    tok = parts.shape[2] // 2
    h = h_own[...]
    u = du[...]
    for n in range(inner):
        cols = slice(n * outer * B, (n + 1) * outer * B)
        to = lax.rem(me[0] + n, inner)
        g = mm(u, wu[:, cols]).astype(BF)
        o = mm(h, wd[:, cols]).astype(BF)
        for j in range(outer):
            parts[to, j, :tok, :] = o[:, j * B : (j + 1) * B]
            parts[to, j, tok:, :] = g[:, j * B : (j + 1) * B]
    done[...] = jnp.zeros_like(done)


def add_up(pieces, at):
    total = pieces[(0,) + at].astype(F32)
    for i in range(1, pieces.shape[0]):
        total += pieces[(i,) + at].astype(F32)
    return total.astype(BF)


def first_sum_kernel(pieces, out):
    for j in range(out.shape[0]):
        out[j] = add_up(pieces, (j,))


def sum_kernel(pieces, mixed, input_grad):
    tok = mixed.shape[0]
    for out, base in ((mixed, 0), (input_grad, tok)):
        for r in range(0, tok, 32):
            out[r : r + 32, :] = add_up(pieces, (slice(base + r, base + r + 32),))


def exchange(x, teams=None):
    return lax.all_to_all(x, "tensor", split_axis=0, concat_axis=0, tiled=True, axis_index_groups=teams)


def turn_kernel(route, came, goes):
    n, rows, lanes = came.shape
    flat = came[...].astype(F32).reshape(n * rows, lanes).astype(BF)
    goes[...] = mm(route[...], flat).reshape(n, rows, lanes).astype(BF)


def shards(
    inner, tokens, gate_pre, up_blocks, up_mask, down_blocks, down_mask, down_owner, cotangent
):
    devices = lax.axis_size("tensor")
    groups = lax.axis_size("dp")
    tok, width = tokens.shape
    hid = gate_pre.shape[1]
    model = devices * width
    kept = up_blocks.shape[1]
    sds = jax.ShapeDtypeStruct

    me = lax.axis_index("tensor").astype(jnp.int32).reshape(1)
    core = lax.bitwise_and(lax.axis_index("dp").astype(jnp.int32), 1).reshape(1)
    tokens, me, core = lax.optimization_barrier((tokens, me, core))
    outer = devices // inner
    along_x = [[z * inner + x for x in range(inner)] for z in range(outer)]
    along_z = [[z * inner + x for z in range(outer)] for x in range(inner)]
    spread = pl.pallas_call(
        spread_kernel,
        out_shape=sds((outer, 2 * tok, width), BF),
        in_specs=[ANY, ANY],
        out_specs=VM,
        scratch_shapes=[
            pltpu.VMEM((tok, width), BF),
            pltpu.VMEM((tok, width), BF),
            pltpu.SemaphoreType.DMA((2,)),
        ],
        compiler_params=params(60),
        name="spread",
    )(tokens, cotangent)
    def shift(x, by):
        pairs = [(z * inner + i, z * inner + (i + by) % inner) for z in range(outer) for i in range(inner)]
        return lax.ppermute(x, "tensor", pairs)

    wu, wd, route, up_pos, down_pos = pl.pallas_call(
        functools.partial(dense_kernel, inner=inner),
        out_shape=(
            sds((hid, model), BF),
            sds((hid, model), BF),
            sds((2 * hid // B * devices, 2 * hid // B * devices), BF),
            sds((kept,), jnp.int32),
            sds((kept,), jnp.int32),
        ),
        in_specs=[SM, SM, SM, SM, VM, ANY],
        out_specs=(VM, VM, VM, SM, SM),
        scratch_shapes=[
            pltpu.VMEM((2 * hid // B * devices, 2 * hid // B * devices), F32),
            pltpu.SMEM((devices,), jnp.int32),
            pltpu.SemaphoreType.DMA((1,)),
        ],
        cost_estimate=pl.CostEstimate(flops=0, bytes_accessed=24 << 20, transcendentals=0),
        compiler_params=params(16),
        name="dense",
    )(me, up_mask, down_mask, down_owner, up_blocks[0], down_blocks[0])

    near = exchange(spread, along_z)
    pieces = [near] + [shift(near, -j) for j in range(1, inner)]
    pairs = [(i, i ^ 1) for i in range(groups)]
    late, up_pos = lax.optimization_barrier((near, up_pos))
    near2 = lax.ppermute(late, "dp", pairs)

    rows = 2 * hid // B
    lanes = tok // devices * B
    up, send, far = pl.pallas_call(
        front_kernel,
        out_shape=(
            sds((tok, hid), F32),
            sds((devices, rows, lanes), BF),
            sds((devices - outer, 2 * tok, width), BF),
        ),
        in_specs=[VM] * 7,
        out_specs=(VM,) * 3,
        scratch_shapes=[
            pltpu.VMEM((hid, tok), F32),
            pltpu.VMEM((tok, hid), F32),
            pltpu.VMEM((devices, rows, lanes), F32),
        ],
        compiler_params=params(16),
        name="front",
    )(*pieces, wu, wd, gate_pre)

    send, near2 = lax.optimization_barrier((send, near2))
    turned = pl.pallas_call(
        turn_kernel,
        out_shape=sds((devices, rows, lanes), BF),
        in_specs=[VM, VM],
        out_specs=VM,
        compiler_params=params(4),
        name="turn",
    )(route, exchange(send))
    got = exchange(turned)
    far2 = lax.ppermute(far, "dp", pairs)

    each = kept // groups
    blocks = hid // B
    gate_grad, du, h_own, swap = pl.pallas_call(
        back_kernel,
        out_shape=(
            sds((tok, hid), BF),
            sds((tok, hid), BF),
            sds((tok, hid), BF),
            sds((2 * blocks, B, B), BF),
        ),
        in_specs=[VM] * 3,
        out_specs=(VM,) * 4,
        scratch_shapes=[pltpu.VMEM((devices, rows, lanes), F32)],
        compiler_params=params(6),
        name="back",
    )(got, up, gate_pre)
    swap2 = lax.ppermute(swap, "dp", pairs)

    parts, done = pl.pallas_call(
        parts_kernel,
        out_shape=(sds((inner, outer, 2 * tok, width), BF), sds((8, B), F32)),
        in_specs=[SM, VM, VM, VM, VM],
        out_specs=(VM, VM),
        compiler_params=params(14),
        cost_estimate=pl.CostEstimate(flops=4 * tok * hid * model, bytes_accessed=10 << 20, transcendentals=0),
        name="parts",
    )(me, h_own, du, wu, wd)
    done, swap2 = lax.optimization_barrier((done, swap2))

    grads = pl.pallas_call(
        grads_kernel,
        out_shape=sds((groups // 2, 2, each, B, B), BF),
        in_specs=[SM] * 3 + [ANY] * 4 + [VM] * 2,
        out_specs=VM,
        scratch_shapes=[
            pltpu.VMEM((devices, 2 * tok, width), BF),
            pltpu.VMEM((devices, 2 * tok, width), BF),
            pltpu.VMEM((blocks, 2 * tok, B), BF),
            pltpu.VMEM((blocks, B, 2 * tok), BF),
            pltpu.SemaphoreType.DMA((4,)),
        ],
        compiler_params=params(12),
        cost_estimate=pl.CostEstimate(flops=2 * kept * 2 * tok * B * B, bytes_accessed=8 << 20, transcendentals=0),
        name="grads",
    )(core, up_pos, down_pos, near, far, near2, far2, swap, swap2)
    parts, grads = lax.optimization_barrier((parts, grads))
    columns = [[y * 2 + c for y in range(groups // 2)] for c in range(2)]
    summed = lax.psum_scatter(grads, "dp", scatter_dimension=0, tiled=True, axis_index_groups=columns)

    first = pl.pallas_call(
        first_sum_kernel,
        out_shape=sds((outer, 2 * tok, width), BF),
        in_specs=[VM],
        out_specs=VM,
        compiler_params=params(8),
        name="first_sums",
    )(exchange(parts, along_x))
    pieces = exchange(first, along_z)
    mixed, input_grad = pl.pallas_call(
        sum_kernel,
        out_shape=(sds((tok, width), BF), sds((tok, width), BF)),
        in_specs=[VM],
        out_specs=(VM, VM),
        compiler_params=params(6),
        name="sums",
    )(pieces)
    return mixed, input_grad, gate_grad, summed[:, 0], summed[:, 1]


def solution(mesh):
    placed = (
        P("dp", "tensor"),
        P("dp", "tensor"),
        P("tensor", None, None, None),
        P(None, "tensor"),
        P("tensor", None, None, None),
        P(),
        P(),
        P("dp", "tensor"),
    )
    return jax.shard_map(
        functools.partial(shards, INNER),
        mesh=mesh,
        in_specs=placed,
        out_specs=(
            P("dp", "tensor"),
            P("dp", "tensor"),
            P("dp", "tensor"),
            P("tensor", "dp", None, None),
            P("tensor", "dp", None, None),
        ),
        check_vma=False,
    )
```

```python
import functools

import jax
import jax.numpy as jnp
from jax import lax
from jax.experimental import pallas as pl
from jax.experimental.pallas import tpu as pltpu
from jax.sharding import PartitionSpec as P


BF = jnp.bfloat16
F32 = jnp.float32
VM = pl.BlockSpec(memory_space=pltpu.VMEM)
SM = pl.BlockSpec(memory_space=pltpu.SMEM)
ANY = pl.BlockSpec(memory_space=pl.ANY)
HBM = pl.BlockSpec(memory_space=pltpu.HBM)


def params(mib):
    return pltpu.CompilerParams(vmem_limit_bytes=mib * 1024 * 1024)


B = 128
INNER = 4


def in_hbm(x):
    return pltpu.with_memory_space_constraint(x, pltpu.HBM)


def mm(a, b, dims=((1,), (0,))):
    return lax.dot_general(a, b, (dims, ((), ())), preferred_element_type=F32)


def dense_kernel(
    me,
    up_mask_in,
    down_mask_in,
    owner_in,
    w_up_in,
    w_down,
    wu,
    wd,
    route,
    up_pos,
    down_pos,
    up_mask,
    down_mask,
    owner,
    w_up,
    ones,
    filled,
    sems,
    inner,
):
    strip, wide = up_mask.shape
    rows = down_mask.shape[1]
    kept = up_pos.shape[0]
    outer = wide // inner
    mine = me[0]
    fetch = pltpu.make_async_copy(w_up_in, w_up, sems.at[1])
    fetch.start()
    lists = [
        pltpu.make_async_copy(src, dst, sems.at[2 + t])
        for t, (src, dst) in enumerate(((up_mask_in, up_mask), (down_mask_in, down_mask), (owner_in, owner)))
    ]
    for copy in lists:
        copy.start()

    def place(r):
        return lax.rem(lax.rem(r, inner) + inner - lax.rem(mine, inner), inner) * outer + r // inner

    for ref in (wu, wd):
        for s in range(strip):
            for c in range(ref.shape[1] // 1024):
                ref[s * B : (s + 1) * B, c * 1024 : (c + 1) * 1024] = jnp.zeros((B, 1024), BF)

    for copy in lists:
        copy.wait()

    def down_row(j, state):
        slot, k = state
        own = owner[j] == mine

        def walk(k):
            s = jnp.minimum(slot, strip - 1)

            def cell(c, k):
                m = down_mask[c, j]

                @pl.when(m > 0)
                def _():
                    kk = jnp.minimum(k, kept - 1)
                    at = place(c)
                    down_pos[kk] = s * wide + at
                    pltpu.make_async_copy(
                        w_down.at[kk],
                        wd.at[pl.ds(pl.multiple_of(s * B, B), B), pl.ds(pl.multiple_of(at * B, B), B)],
                        sems.at[0],
                    ).start()

                return k + jnp.where(m > 0, 1, 0)

            return lax.fori_loop(0, wide, cell, k)

        k = lax.cond(own, walk, lambda k: k, k)
        return slot + jnp.where(own, 1, 0), k

    lax.fori_loop(0, rows, down_row, (0, 0))

    def up_step(r, k):
        at = place(r) * strip
        for c in range(strip):
            m = up_mask[c, r]

            @pl.when(m > 0)
            def _(k=k, c=c):
                up_pos[jnp.minimum(k, kept - 1)] = at + c

            k = k + jnp.where(m > 0, 1, 0)
        return k

    lax.fori_loop(0, wide, up_step, 0)

    def turn(i, carry):
        for j in range(8):
            k = i * 8 + j
            p = up_pos[k]
            r = pl.multiple_of(p // strip * B, B)
            c = pl.multiple_of(lax.rem(p, strip) * B, B)
            wu[pl.ds(c, B), pl.ds(r, B)] = w_up[k].T
        return carry

    fetch.wait()
    lax.fori_loop(0, kept // 8, turn, 0)

    for t in range(wide):
        filled[t] = 0
    lane = lax.broadcasted_iota(jnp.int32, (1, ones.shape[1]), 1)

    def line(i, carry):
        to = jnp.clip(owner[i], 0, wide - 1)
        n = jnp.minimum(filled[to], strip - 1)
        filled[to] = n + 1
        there = to * 2 * strip + n
        here = i // strip * 2 * strip + lax.rem(i, strip)
        ones[pl.ds(there, 1), :] = jnp.where(lane == here, 1.0, 0.0)
        ones[pl.ds(here + strip, 1), :] = jnp.where(lane == there + strip, 1.0, 0.0)
        return carry

    lax.fori_loop(0, rows, line, 0)
    route[...] = ones[...].astype(BF)
    pltpu.make_async_copy(w_down, w_down, sems.at[0]).wait()


def front_kernel(r0, r1, r2, r3, wu, wd, gate, up_ref, send, far, acc_u, acc, wide):
    outer, tok = r0.shape[0], r0.shape[1] // 2
    hid = wu.shape[0]
    for n, recv in enumerate((r0, r1, r2, r3)):
        if n > 0:
            far[(n - 1) * outer : n * outer] = recv[...]
        cols = slice(n * outer * B, (n + 1) * outer * B)
        x = jnp.concatenate([recv[i, :tok, :] for i in range(outer)], axis=0)
        y = jnp.concatenate([recv[i, tok:, :] for i in range(outer)], axis=1)
        u = mm(wu[:, cols], x)
        d = mm(y, wd[:, cols], ((1,), (1,)))
        if n == 0:
            acc_u[...] = u
            acc[...] = d
        else:
            acc_u[...] += u
            acc[...] += d
    for b in range(hid // B):
        up_ref[:, b * B : (b + 1) * B] = acc_u[b * B : (b + 1) * B, :].T
    slices = send.shape[0]
    blocks = hid // B
    per = tok // slices
    for b in range(blocks):
        cols = slice(b * B, (b + 1) * B)
        g = gate[:, cols].astype(F32)
        h = (g * jax.nn.sigmoid(g) * up_ref[:, cols]).astype(BF).astype(F32)
        d = acc[:, cols].astype(BF).astype(F32)
        for q in range(per):
            rows = slice(q * slices, (q + 1) * slices)
            wide[:, b, q * B : (q + 1) * B] = h[rows, :]
            wide[:, blocks + b, q * B : (q + 1) * B] = d[rows, :]
    send[...] = wide[...].astype(BF)


def spread_kernel(tokens_in, cotangent_in, out, tokens, cotangent, sems):
    width = tokens.shape[1]
    first = pltpu.make_async_copy(tokens_in, tokens, sems.at[0])
    second = pltpu.make_async_copy(cotangent_in, cotangent, sems.at[1])
    first.start()
    second.start()
    first.wait()
    second.wait()
    x = tokens[...].astype(F32).T.astype(BF)
    y = cotangent[...]
    for i in range(out.shape[0]):
        out[i, :width, :] = x
        out[i, width:, :] = y


def back_kernel(got, up_ref, gate, gate_grad, du, h_own, swap, wide):
    slices = got.shape[0]
    blocks = gate.shape[1] // B
    per = gate.shape[0] // slices
    wide[...] = got[...].astype(F32)
    for b in range(blocks):
        cols = slice(b * B, (b + 1) * B)
        h = jnp.concatenate([wide[:, b, q * B : (q + 1) * B] for q in range(per)], axis=0)
        d = jnp.concatenate([wide[:, blocks + b, q * B : (q + 1) * B] for q in range(per)], axis=0)
        h_own[:, cols] = h.astype(BF)
        swap[blocks + b] = h.T.astype(BF)
        g = gate[:, cols].astype(F32)
        s = jax.nn.sigmoid(g)
        gate_grad[:, cols] = (d * up_ref[:, cols] * s * (1.0 + g * (1.0 - s))).astype(BF)
        u = (d * (g * s)).astype(BF)
        du[:, cols] = u
        swap[b] = u


def grads_kernel(core, up_pos, down_pos, near, far, near2, far2, swap, swap2, grads, full, full2, du, ht, sems):
    outer = near.shape[0]
    n_src = full.shape[0]
    tok = full.shape[1] // 2
    blocks = du.shape[0]
    moves = []
    for t, (src, dst) in enumerate(
        ((near, full.at[:outer]), (far, full.at[outer:]), (near2, full2.at[:outer]), (far2, full2.at[outer:]))
    ):
        move = pltpu.make_async_copy(src, dst, sems.at[t])
        move.start()
        moves.append(move)
    for b in range(blocks):
        du[b, :tok, :] = swap[b]
        du[b, tok:, :] = swap2[b]
        ht[b, :, :tok] = swap[blocks + b]
        ht[b, :, tok:] = swap2[blocks + b]
    for move in moves:
        move.wait()
    each = grads.shape[2]

    def block(i, c):
        for j in range(each):
            k = (2 * i + core[0]) * each + j
            p = up_pos[k]
            r = p // blocks
            xt = jnp.concatenate([full[r, :tok, :], full2[r, :tok, :]], axis=1)
            grads[i, 0, j] = mm(xt, du[lax.rem(p, blocks)]).astype(BF)
            p = down_pos[k]
            r = lax.rem(p, n_src)
            y = jnp.concatenate([full[r, tok:, :], full2[r, tok:, :]], axis=0)
            grads[i, 1, j] = mm(ht[p // n_src], y).astype(BF)
        return c

    lax.fori_loop(0, grads.shape[0], block, 0)


def parts_kernel(me, h_own, du, wu, wd, parts, done):
    inner, outer = parts.shape[:2]
    tok = parts.shape[2] // 2
    h = h_own[...]
    u = du[...]
    for n in range(inner):
        cols = slice(n * outer * B, (n + 1) * outer * B)
        to = lax.rem(me[0] + n, inner)
        g = mm(u, wu[:, cols]).astype(BF)
        o = mm(h, wd[:, cols]).astype(BF)
        for j in range(outer):
            parts[to, j, :tok, :] = o[:, j * B : (j + 1) * B]
            parts[to, j, tok:, :] = g[:, j * B : (j + 1) * B]
    done[...] = jnp.zeros_like(done)


def add_up(pieces, at):
    total = pieces[(0,) + at].astype(F32)
    for i in range(1, pieces.shape[0]):
        total += pieces[(i,) + at].astype(F32)
    return total.astype(BF)


def first_sum_kernel(pieces, out):
    for j in range(out.shape[0]):
        out[j] = add_up(pieces, (j,))


def sum_kernel(pieces, summed, mixed, input_grad, up_grad, down_grad, sems):
    moves = [
        pltpu.make_async_copy(summed.at[:, t], out, sems.at[t]) for t, out in enumerate((up_grad, down_grad))
    ]
    for move in moves:
        move.start()
    tok = mixed.shape[0]
    for out, base in ((mixed, 0), (input_grad, tok)):
        for r in range(0, tok, 32):
            out[r : r + 32, :] = add_up(pieces, (slice(base + r, base + r + 32),))
    for move in moves:
        move.wait()


def exchange(x, teams=None):
    return lax.all_to_all(x, "tensor", split_axis=0, concat_axis=0, tiled=True, axis_index_groups=teams)


def turn_kernel(route, came, goes):
    n, rows, lanes = came.shape
    flat = came[...].astype(F32).reshape(n * rows, lanes).astype(BF)
    goes[...] = mm(route[...], flat).reshape(n, rows, lanes).astype(BF)


def shards(
    inner, tokens, gate_pre, up_blocks, up_mask, down_blocks, down_mask, down_owner, cotangent
):
    devices = lax.axis_size("tensor")
    groups = lax.axis_size("dp")
    tok, width = tokens.shape
    hid = gate_pre.shape[1]
    model = devices * width
    kept = up_blocks.shape[1]
    sds = jax.ShapeDtypeStruct

    me = lax.axis_index("tensor").astype(jnp.int32).reshape(1)
    core = lax.bitwise_and(lax.axis_index("dp").astype(jnp.int32), 1).reshape(1)
    tokens, me, core = lax.optimization_barrier((tokens, me, core))
    outer = devices // inner
    along_x = [[z * inner + x for x in range(inner)] for z in range(outer)]
    along_z = [[z * inner + x for z in range(outer)] for x in range(inner)]
    spread = pl.pallas_call(
        spread_kernel,
        out_shape=sds((outer, 2 * tok, width), BF),
        in_specs=[HBM, HBM],
        out_specs=VM,
        scratch_shapes=[
            pltpu.VMEM((tok, width), BF),
            pltpu.VMEM((tok, width), BF),
            pltpu.SemaphoreType.DMA((2,)),
        ],
        compiler_params=params(6),
        name="spread",
    )(in_hbm(tokens), in_hbm(cotangent))
    def shift(x, by):
        pairs = [(z * inner + i, z * inner + (i + by) % inner) for z in range(outer) for i in range(inner)]
        return lax.ppermute(x, "tensor", pairs)

    wu, wd, route, up_pos, down_pos = pl.pallas_call(
        functools.partial(dense_kernel, inner=inner),
        out_shape=(
            sds((hid, model), BF),
            sds((hid, model), BF),
            sds((2 * hid // B * devices, 2 * hid // B * devices), BF),
            sds((kept,), jnp.int32),
            sds((kept,), jnp.int32),
        ),
        in_specs=[SM, HBM, HBM, HBM, HBM, HBM],
        out_specs=(VM, VM, VM, SM, SM),
        scratch_shapes=[
            pltpu.SMEM(up_mask.T.shape, jnp.int32),
            pltpu.SMEM(down_mask.T.shape, jnp.int32),
            pltpu.SMEM(down_owner.shape, jnp.int32),
            pltpu.VMEM((kept, B, B), BF),
            pltpu.VMEM((2 * hid // B * devices, 2 * hid // B * devices), F32),
            pltpu.SMEM((devices,), jnp.int32),
            pltpu.SemaphoreType.DMA((5,)),
        ],
        cost_estimate=pl.CostEstimate(flops=0, bytes_accessed=24 << 20, transcendentals=0),
        compiler_params=params(16),
        name="dense",
    )(
        me,
        in_hbm(up_mask.T),
        in_hbm(down_mask.T),
        in_hbm(down_owner),
        in_hbm(up_blocks[0]),
        in_hbm(down_blocks[0]),
    )

    near = exchange(spread, along_z)
    pieces = [near] + [shift(near, -j) for j in range(1, inner)]
    pairs = [(i, i ^ 1) for i in range(groups)]
    late, up_pos = lax.optimization_barrier((near, up_pos))
    near2 = lax.ppermute(late, "dp", pairs)

    rows = 2 * hid // B
    lanes = tok // devices * B
    up, send, far = pl.pallas_call(
        front_kernel,
        out_shape=(
            sds((tok, hid), F32),
            sds((devices, rows, lanes), BF),
            sds((devices - outer, 2 * tok, width), BF),
        ),
        in_specs=[VM] * 7,
        out_specs=(VM,) * 3,
        scratch_shapes=[
            pltpu.VMEM((hid, tok), F32),
            pltpu.VMEM((tok, hid), F32),
            pltpu.VMEM((devices, rows, lanes), F32),
        ],
        compiler_params=params(16),
        name="front",
    )(*pieces, wu, wd, gate_pre)

    send, near2 = lax.optimization_barrier((send, near2))
    turned = pl.pallas_call(
        turn_kernel,
        out_shape=sds((devices, rows, lanes), BF),
        in_specs=[VM, VM],
        out_specs=VM,
        compiler_params=params(4),
        name="turn",
    )(route, exchange(send))
    got = exchange(turned)
    far2 = lax.ppermute(far, "dp", pairs)

    each = kept // groups
    blocks = hid // B
    gate_grad, du, h_own, swap = pl.pallas_call(
        back_kernel,
        out_shape=(
            sds((tok, hid), BF),
            sds((tok, hid), BF),
            sds((tok, hid), BF),
            sds((2 * blocks, B, B), BF),
        ),
        in_specs=[VM] * 3,
        out_specs=(VM,) * 4,
        scratch_shapes=[pltpu.VMEM((devices, rows, lanes), F32)],
        compiler_params=params(6),
        name="back",
    )(got, up, gate_pre)
    swap2 = lax.ppermute(swap, "dp", pairs)

    parts, done = pl.pallas_call(
        parts_kernel,
        out_shape=(sds((inner, outer, 2 * tok, width), BF), sds((8, B), F32)),
        in_specs=[SM, VM, VM, VM, VM],
        out_specs=(VM, VM),
        compiler_params=params(14),
        cost_estimate=pl.CostEstimate(flops=4 * tok * hid * model, bytes_accessed=10 << 20, transcendentals=0),
        name="parts",
    )(me, h_own, du, wu, wd)
    done, swap2 = lax.optimization_barrier((done, swap2))

    grads = pl.pallas_call(
        grads_kernel,
        out_shape=sds((groups // 2, 2, each, B, B), BF),
        in_specs=[SM] * 3 + [ANY] * 4 + [VM] * 2,
        out_specs=VM,
        scratch_shapes=[
            pltpu.VMEM((devices, 2 * tok, width), BF),
            pltpu.VMEM((devices, 2 * tok, width), BF),
            pltpu.VMEM((blocks, 2 * tok, B), BF),
            pltpu.VMEM((blocks, B, 2 * tok), BF),
            pltpu.SemaphoreType.DMA((4,)),
        ],
        compiler_params=params(12),
        cost_estimate=pl.CostEstimate(flops=2 * kept * 2 * tok * B * B, bytes_accessed=8 << 20, transcendentals=0),
        name="grads",
    )(core, up_pos, down_pos, near, far, near2, far2, swap, swap2)
    parts, grads = lax.optimization_barrier((parts, grads))
    columns = [[y * 2 + c for y in range(groups // 2)] for c in range(2)]
    summed = lax.psum_scatter(grads, "dp", scatter_dimension=0, tiled=True, axis_index_groups=columns)

    first = pl.pallas_call(
        first_sum_kernel,
        out_shape=sds((outer, 2 * tok, width), BF),
        in_specs=[VM],
        out_specs=VM,
        compiler_params=params(8),
        name="first_sums",
    )(exchange(parts, along_x))
    pieces = exchange(first, along_z)
    shared = sds((1, each, B, B), BF)
    mixed, input_grad, up_grad, down_grad = pl.pallas_call(
        sum_kernel,
        out_shape=(sds((tok, width), BF), sds((tok, width), BF), shared, shared),
        in_specs=[VM, HBM],
        out_specs=(VM, VM, ANY, ANY),
        scratch_shapes=[pltpu.SemaphoreType.DMA((2,))],
        compiler_params=params(6),
        name="sums",
    )(pieces, in_hbm(summed))
    return mixed, input_grad, gate_grad, up_grad, down_grad


def solution(mesh):
    placed = (
        P("dp", "tensor"),
        P("dp", "tensor"),
        P("tensor", None, None, None),
        P(None, "tensor"),
        P("tensor", None, None, None),
        P(),
        P(),
        P("dp", "tensor"),
    )
    return jax.shard_map(
        functools.partial(shards, INNER),
        mesh=mesh,
        in_specs=placed,
        out_specs=(
            P("dp", "tensor"),
            P("dp", "tensor"),
            P("dp", "tensor"),
            P("tensor", "dp", None, None),
            P("tensor", "dp", None, None),
        ),
        check_vma=False,
    )
```

```python
import functools

import jax
import jax.numpy as jnp
from jax import lax
from jax.experimental import pallas as pl
from jax.experimental.pallas import tpu as pltpu
from jax.sharding import PartitionSpec as P


BF = jnp.bfloat16
F32 = jnp.float32
VM = pl.BlockSpec(memory_space=pltpu.VMEM)
SM = pl.BlockSpec(memory_space=pltpu.SMEM)
ANY = pl.BlockSpec(memory_space=pl.ANY)
HBM = pl.BlockSpec(memory_space=pltpu.HBM)


def params(mib):
    return pltpu.CompilerParams(vmem_limit_bytes=mib * 1024 * 1024)


B = 128
INNER = 4


def in_hbm(x):
    return pltpu.with_memory_space_constraint(x, pltpu.HBM)


def mm(a, b, dims=((1,), (0,))):
    return lax.dot_general(a, b, (dims, ((), ())), preferred_element_type=F32)


def dense_kernel(
    me,
    up_mask_in,
    down_mask_in,
    owner_in,
    w_up_in,
    w_down,
    wu,
    wd,
    route,
    up_pos,
    down_pos,
    up_mask,
    down_mask,
    owner,
    w_up,
    ones,
    filled,
    sems,
    inner,
):
    strip, wide = up_mask.shape
    rows = down_mask.shape[1]
    kept = up_pos.shape[0]
    outer = wide // inner
    mine = me[0]
    fetch = pltpu.make_async_copy(w_up_in, w_up, sems.at[1])
    fetch.start()
    lists = [
        pltpu.make_async_copy(src, dst, sems.at[2 + t])
        for t, (src, dst) in enumerate(((up_mask_in, up_mask), (down_mask_in, down_mask), (owner_in, owner)))
    ]
    for copy in lists:
        copy.start()

    def place(r):
        return lax.rem(lax.rem(r, inner) + inner - lax.rem(mine, inner), inner) * outer + r // inner

    for ref in (wu, wd):
        for s in range(strip):
            for c in range(ref.shape[1] // 1024):
                ref[s * B : (s + 1) * B, c * 1024 : (c + 1) * 1024] = jnp.zeros((B, 1024), BF)

    for copy in lists:
        copy.wait()

    def down_row(j, state):
        slot, k = state
        own = owner[j] == mine

        def walk(k):
            s = jnp.minimum(slot, strip - 1)

            def cell(c, k):
                m = down_mask[c, j]

                @pl.when(m > 0)
                def _():
                    kk = jnp.minimum(k, kept - 1)
                    at = place(c)
                    down_pos[kk] = s * wide + at
                    pltpu.make_async_copy(
                        w_down.at[kk],
                        wd.at[pl.ds(pl.multiple_of(s * B, B), B), pl.ds(pl.multiple_of(at * B, B), B)],
                        sems.at[0],
                    ).start()

                return k + jnp.where(m > 0, 1, 0)

            return lax.fori_loop(0, wide, cell, k)

        k = lax.cond(own, walk, lambda k: k, k)
        return slot + jnp.where(own, 1, 0), k

    lax.fori_loop(0, rows, down_row, (0, 0))

    def up_step(r, k):
        at = place(r) * strip
        for c in range(strip):
            m = up_mask[c, r]

            @pl.when(m > 0)
            def _(k=k, c=c):
                up_pos[jnp.minimum(k, kept - 1)] = at + c

            k = k + jnp.where(m > 0, 1, 0)
        return k

    lax.fori_loop(0, wide, up_step, 0)

    def turn(i, carry):
        for j in range(8):
            k = i * 8 + j
            p = up_pos[k]
            r = pl.multiple_of(p // strip * B, B)
            c = pl.multiple_of(lax.rem(p, strip) * B, B)
            wu[pl.ds(c, B), pl.ds(r, B)] = w_up[k].T
        return carry

    fetch.wait()
    lax.fori_loop(0, kept // 8, turn, 0)

    for t in range(wide):
        filled[t] = 0
    lane = lax.broadcasted_iota(jnp.int32, (1, ones.shape[1]), 1)

    def line(i, carry):
        to = jnp.clip(owner[i], 0, wide - 1)
        n = jnp.minimum(filled[to], strip - 1)
        filled[to] = n + 1
        there = to * 2 * strip + n
        here = i // strip * 2 * strip + lax.rem(i, strip)
        ones[pl.ds(there, 1), :] = jnp.where(lane == here, 1.0, 0.0)
        ones[pl.ds(here + strip, 1), :] = jnp.where(lane == there + strip, 1.0, 0.0)
        return carry

    lax.fori_loop(0, rows, line, 0)
    route[...] = ones[...].astype(BF)
    pltpu.make_async_copy(w_down, w_down, sems.at[0]).wait()


def front_kernel(r0, r1, r2, r3, wu, wd, gate, up_ref, send, far, acc_u, acc, wide):
    outer, tok = r0.shape[0], r0.shape[1] // 2
    hid = wu.shape[0]
    for n, recv in enumerate((r0, r1, r2, r3)):
        if n > 0:
            far[(n - 1) * outer : n * outer] = recv[...]
        cols = slice(n * outer * B, (n + 1) * outer * B)
        x = jnp.concatenate([recv[i, :tok, :] for i in range(outer)], axis=0)
        y = jnp.concatenate([recv[i, tok:, :] for i in range(outer)], axis=1)
        u = mm(wu[:, cols], x)
        d = mm(y, wd[:, cols], ((1,), (1,)))
        if n == 0:
            acc_u[...] = u
            acc[...] = d
        else:
            acc_u[...] += u
            acc[...] += d
    for b in range(hid // B):
        up_ref[:, b * B : (b + 1) * B] = acc_u[b * B : (b + 1) * B, :].T
    slices = send.shape[0]
    blocks = hid // B
    per = tok // slices
    for b in range(blocks):
        cols = slice(b * B, (b + 1) * B)
        g = gate[:, cols].astype(F32)
        h = (g * jax.nn.sigmoid(g) * up_ref[:, cols]).astype(BF).astype(F32)
        d = acc[:, cols].astype(BF).astype(F32)
        for q in range(per):
            rows = slice(q * slices, (q + 1) * slices)
            wide[:, b, q * B : (q + 1) * B] = h[rows, :]
            wide[:, blocks + b, q * B : (q + 1) * B] = d[rows, :]
    send[...] = wide[...].astype(BF)


def spread_kernel(tokens_in, cotangent_in, out, tokens, cotangent, sems):
    width = tokens.shape[1]
    first = pltpu.make_async_copy(tokens_in, tokens, sems.at[0])
    second = pltpu.make_async_copy(cotangent_in, cotangent, sems.at[1])
    first.start()
    second.start()
    first.wait()
    second.wait()
    x = tokens[...].astype(F32).T.astype(BF)
    y = cotangent[...]
    for i in range(out.shape[0]):
        out[i, :width, :] = x
        out[i, width:, :] = y


def back_kernel(got, up_ref, gate, gate_grad, du, h_own, swap, wide):
    slices = got.shape[0]
    blocks = gate.shape[1] // B
    per = gate.shape[0] // slices
    wide[...] = got[...].astype(F32)
    for b in range(blocks):
        cols = slice(b * B, (b + 1) * B)
        h = jnp.concatenate([wide[:, b, q * B : (q + 1) * B] for q in range(per)], axis=0)
        d = jnp.concatenate([wide[:, blocks + b, q * B : (q + 1) * B] for q in range(per)], axis=0)
        h_own[:, cols] = h.astype(BF)
        swap[blocks + b] = h.T.astype(BF)
        g = gate[:, cols].astype(F32)
        s = jax.nn.sigmoid(g)
        gate_grad[:, cols] = (d * up_ref[:, cols] * s * (1.0 + g * (1.0 - s))).astype(BF)
        u = (d * (g * s)).astype(BF)
        du[:, cols] = u
        swap[b] = u


def grads_kernel(core, up_pos, down_pos, near, far, near2, far2, swap, swap2, grads, full, full2, du, ht, sems):
    outer = near.shape[0]
    n_src = full.shape[0]
    tok = full.shape[1] // 2
    blocks = du.shape[0]
    moves = []
    for t, (src, dst) in enumerate(
        ((near, full.at[:outer]), (far, full.at[outer:]), (near2, full2.at[:outer]), (far2, full2.at[outer:]))
    ):
        move = pltpu.make_async_copy(src, dst, sems.at[t])
        move.start()
        moves.append(move)
    for b in range(blocks):
        du[b, :tok, :] = swap[b]
        du[b, tok:, :] = swap2[b]
        ht[b, :, :tok] = swap[blocks + b]
        ht[b, :, tok:] = swap2[blocks + b]
    for move in moves:
        move.wait()
    each = grads.shape[2]

    def block(i, c):
        for j in range(each):
            k = (2 * i + core[0]) * each + j
            p = up_pos[k]
            r = p // blocks
            xt = jnp.concatenate([full[r, :tok, :], full2[r, :tok, :]], axis=1)
            grads[i, 0, j] = mm(xt, du[lax.rem(p, blocks)]).astype(BF)
            p = down_pos[k]
            r = lax.rem(p, n_src)
            y = jnp.concatenate([full[r, tok:, :], full2[r, tok:, :]], axis=0)
            grads[i, 1, j] = mm(ht[p // n_src], y).astype(BF)
        return c

    lax.fori_loop(0, grads.shape[0], block, 0)


def parts_kernel(me, h_own, du, wu, wd, parts, done):
    inner, outer = parts.shape[:2]
    tok = parts.shape[2] // 2
    h = h_own[...]
    u = du[...]
    for n in range(inner):
        cols = slice(n * outer * B, (n + 1) * outer * B)
        to = lax.rem(me[0] + n, inner)
        g = mm(u, wu[:, cols]).astype(BF)
        o = mm(h, wd[:, cols]).astype(BF)
        for j in range(outer):
            parts[to, j, :tok, :] = o[:, j * B : (j + 1) * B]
            parts[to, j, tok:, :] = g[:, j * B : (j + 1) * B]
    done[...] = jnp.zeros_like(done)


def add_up(pieces, at):
    total = pieces[(0,) + at].astype(F32)
    for i in range(1, pieces.shape[0]):
        total += pieces[(i,) + at].astype(F32)
    return total.astype(BF)


def first_sum_kernel(pieces, out):
    for j in range(out.shape[0]):
        out[j] = add_up(pieces, (j,))


def sum_kernel(pieces, summed, mixed, input_grad, up_grad, down_grad, sems):
    moves = [
        pltpu.make_async_copy(summed.at[:, t], out, sems.at[t]) for t, out in enumerate((up_grad, down_grad))
    ]
    for move in moves:
        move.start()
    tok = mixed.shape[0]
    for out, base in ((mixed, 0), (input_grad, tok)):
        for r in range(0, tok, 32):
            out[r : r + 32, :] = add_up(pieces, (slice(base + r, base + r + 32),))
    for move in moves:
        move.wait()


def exchange(x, teams=None):
    return lax.all_to_all(x, "tensor", split_axis=0, concat_axis=0, tiled=True, axis_index_groups=teams)


def turn_kernel(route, came, goes):
    n, rows, lanes = came.shape
    flat = came[...].astype(F32).reshape(n * rows, lanes).astype(BF)
    goes[...] = mm(route[...], flat).reshape(n, rows, lanes).astype(BF)


def shards(
    inner, tokens, gate_pre, up_blocks, up_mask, down_blocks, down_mask, down_owner, cotangent
):
    devices = lax.axis_size("tensor")
    groups = lax.axis_size("dp")
    tok, width = tokens.shape
    hid = gate_pre.shape[1]
    model = devices * width
    kept = up_blocks.shape[1]
    sds = jax.ShapeDtypeStruct

    me = lax.axis_index("tensor").astype(jnp.int32).reshape(1)
    core = lax.bitwise_and(lax.axis_index("dp").astype(jnp.int32), 1).reshape(1)
    tokens, me, core = lax.optimization_barrier((tokens, me, core))
    outer = devices // inner
    along_x = [[z * inner + x for x in range(inner)] for z in range(outer)]
    along_z = [[z * inner + x for z in range(outer)] for x in range(inner)]
    spread = pl.pallas_call(
        spread_kernel,
        out_shape=sds((outer, 2 * tok, width), BF),
        in_specs=[HBM, HBM],
        out_specs=VM,
        scratch_shapes=[
            pltpu.VMEM((tok, width), BF),
            pltpu.VMEM((tok, width), BF),
            pltpu.SemaphoreType.DMA((2,)),
        ],
        compiler_params=params(6),
        name="spread",
    )(in_hbm(tokens), in_hbm(cotangent))
    def shift(x, by):
        pairs = [(z * inner + i, z * inner + (i + by) % inner) for z in range(outer) for i in range(inner)]
        return lax.ppermute(x, "tensor", pairs)

    wu, wd, route, up_pos, down_pos = pl.pallas_call(
        functools.partial(dense_kernel, inner=inner),
        out_shape=(
            sds((hid, model), BF),
            sds((hid, model), BF),
            sds((2 * hid // B * devices, 2 * hid // B * devices), BF),
            sds((kept,), jnp.int32),
            sds((kept,), jnp.int32),
        ),
        in_specs=[SM, HBM, HBM, HBM, HBM, HBM],
        out_specs=(VM, VM, VM, SM, SM),
        scratch_shapes=[
            pltpu.SMEM(up_mask.T.shape, jnp.int32),
            pltpu.SMEM(down_mask.T.shape, jnp.int32),
            pltpu.SMEM(down_owner.shape, jnp.int32),
            pltpu.VMEM((kept, B, B), BF),
            pltpu.VMEM((2 * hid // B * devices, 2 * hid // B * devices), F32),
            pltpu.SMEM((devices,), jnp.int32),
            pltpu.SemaphoreType.DMA((5,)),
        ],
        cost_estimate=pl.CostEstimate(flops=0, bytes_accessed=24 << 20, transcendentals=0),
        compiler_params=params(16),
        name="dense",
    )(
        me,
        in_hbm(up_mask.T),
        in_hbm(down_mask.T),
        in_hbm(down_owner),
        in_hbm(up_blocks[0]),
        in_hbm(down_blocks[0]),
    )

    near = exchange(spread, along_z)
    pieces = [near] + [shift(near, -j) for j in range(1, inner)]
    pairs = [(i, i ^ 1) for i in range(groups)]
    late, up_pos = lax.optimization_barrier((near, up_pos))
    near2 = lax.ppermute(late, "dp", pairs)

    rows = 2 * hid // B
    lanes = tok // devices * B
    up, send, far = pl.pallas_call(
        front_kernel,
        out_shape=(
            sds((tok, hid), F32),
            sds((devices, rows, lanes), BF),
            sds((devices - outer, 2 * tok, width), BF),
        ),
        in_specs=[VM] * 7,
        out_specs=(VM,) * 3,
        scratch_shapes=[
            pltpu.VMEM((hid, tok), F32),
            pltpu.VMEM((tok, hid), F32),
            pltpu.VMEM((devices, rows, lanes), F32),
        ],
        compiler_params=params(16),
        name="front",
    )(*pieces, wu, wd, gate_pre)

    send, near2 = lax.optimization_barrier((send, near2))
    turned = pl.pallas_call(
        turn_kernel,
        out_shape=sds((devices, rows, lanes), BF),
        in_specs=[VM, VM],
        out_specs=VM,
        compiler_params=params(4),
        name="turn",
    )(route, exchange(send))
    got = exchange(turned)
    far2 = lax.ppermute(far, "dp", pairs)

    each = kept // groups
    blocks = hid // B
    gate_grad, du, h_own, swap = pl.pallas_call(
        back_kernel,
        out_shape=(
            sds((tok, hid), BF),
            sds((tok, hid), BF),
            sds((tok, hid), BF),
            sds((2 * blocks, B, B), BF),
        ),
        in_specs=[VM] * 3,
        out_specs=(VM,) * 4,
        scratch_shapes=[pltpu.VMEM((devices, rows, lanes), F32)],
        compiler_params=params(6),
        name="back",
    )(got, up, gate_pre)
    swap2 = lax.ppermute(swap, "dp", pairs)

    parts, done = pl.pallas_call(
        parts_kernel,
        out_shape=(sds((inner, outer, 2 * tok, width), BF), sds((8, B), F32)),
        in_specs=[SM, VM, VM, VM, VM],
        out_specs=(VM, VM),
        compiler_params=params(14),
        cost_estimate=pl.CostEstimate(flops=4 * tok * hid * model, bytes_accessed=10 << 20, transcendentals=0),
        name="parts",
    )(me, h_own, du, wu, wd)
    done, swap2 = lax.optimization_barrier((done, swap2))

    grads = pl.pallas_call(
        grads_kernel,
        out_shape=sds((groups // 2, 2, each, B, B), BF),
        in_specs=[SM] * 3 + [ANY] * 4 + [VM] * 2,
        out_specs=VM,
        scratch_shapes=[
            pltpu.VMEM((devices, 2 * tok, width), BF),
            pltpu.VMEM((devices, 2 * tok, width), BF),
            pltpu.VMEM((blocks, 2 * tok, B), BF),
            pltpu.VMEM((blocks, B, 2 * tok), BF),
            pltpu.SemaphoreType.DMA((4,)),
        ],
        compiler_params=params(12),
        cost_estimate=pl.CostEstimate(flops=2 * kept * 2 * tok * B * B, bytes_accessed=8 << 20, transcendentals=0),
        name="grads",
    )(core, up_pos, down_pos, near, far, near2, far2, swap, swap2)
    parts, grads = lax.optimization_barrier((parts, grads))
    columns = [[y * 2 + c for y in range(groups // 2)] for c in range(2)]
    summed = lax.psum_scatter(grads, "dp", scatter_dimension=0, tiled=True, axis_index_groups=columns)

    first = pl.pallas_call(
        first_sum_kernel,
        out_shape=sds((outer, 2 * tok, width), BF),
        in_specs=[VM],
        out_specs=VM,
        compiler_params=params(8),
        name="first_sums",
    )(exchange(parts, along_x))
    pieces = exchange(first, along_z)
    shared = sds((1, each, B, B), BF)
    mixed, input_grad, up_grad, down_grad = pl.pallas_call(
        sum_kernel,
        out_shape=(sds((tok, width), BF), sds((tok, width), BF), shared, shared),
        in_specs=[VM, HBM],
        out_specs=(VM,) * 4,
        scratch_shapes=[pltpu.SemaphoreType.DMA((2,))],
        compiler_params=params(6),
        name="sums",
    )(pieces, in_hbm(summed))
    return mixed, input_grad, gate_grad, up_grad, down_grad


def solution(mesh):
    placed = (
        P("dp", "tensor"),
        P("dp", "tensor"),
        P("tensor", None, None, None),
        P(None, "tensor"),
        P("tensor", None, None, None),
        P(),
        P(),
        P("dp", "tensor"),
    )
    return jax.shard_map(
        functools.partial(shards, INNER),
        mesh=mesh,
        in_specs=placed,
        out_specs=(
            P("dp", "tensor"),
            P("dp", "tensor"),
            P("dp", "tensor"),
            P("tensor", "dp", None, None),
            P("tensor", "dp", None, None),
        ),
        check_vma=False,
    )
```
